32 devices in a mesh: groups: 2 (over x), tok: 16 (over z, y, core).
Axes of the slice: x: 2, y: 2, z: 4, core: 2. Of those that a mesh axis runs over, the one named last changes fastest.
Arguments:
- taps: bfloat16 [512, 12288], P('groups', 'tok'), parts along dimension 0, may hold values from -6 to 6
- w_join: bfloat16 [12288, 4096], P('tok'), may hold values from -0.0546875 to 0.0546875
- w_down: bfloat16 [4096, 64], replicated, may hold values from -0.09375 to 0.09375
- w_up: bfloat16 [64, 4096], replicated, may hold values from -0.75 to 0.75
- upstream: bfloat16 [512, 12288], P(('groups', 'tok')), parts along dimension 0, may hold values from -6 to 6
Outputs:
- drafts: bfloat16 [512, 12288], P(('groups', 'tok')), parts along dimension 0
- join_grad: float32 [12288, 8192], P('tok', 'groups'), parts along dimension 1
- down_grad: float32 [8192, 64], P('groups'), parts along dimension 0
- up_grad: float32 [128, 4096], P('groups'), parts along dimension 0
The draws below stay inside these ranges and needn't reach their ends.
There are 2 independent parts, one for each index of `groups`. The reference program is written for one: setup_inputs(seed, part) draws one part's arguments, and reference() takes and returns one part's arrays. A program takes and returns all parts, laid end to end along the dimension named above; an argument that names none is the same for every part. Nothing has to cross between parts.
All inputs are finite; a program needn't handle non-finite values.
Results may differ from the reference program's by a relative error of at most 0.008.
Values may be sent and summed in bfloat16 or wider, within the bound.
A program may use at most 128 MiB of HBM per device.

```python
import jax
import jax.numpy as jnp
from jax import lax

HID = 4096
RANK = 64
STEPS = 3
TOKENS = 256
TAPS = 12288


def with_spikes(array, key, source, target, blocks, factor):
    def block_of(dim):
        return (jnp.arange(array.shape[dim]) // (array.shape[dim] // blocks)).reshape((-1,) + (1,) * (array.ndim - 1 - dim))

    near = jax.random.permutation(key, blocks)[block_of(target)]
    second = (block_of(target) + blocks // 2) % blocks
    return jnp.where((block_of(source) == near) | (block_of(source) == second), factor * array, array)


def steps_of(rng, shape, split, low, top_value):
    loudness, own = 1.0, jax.random.fold_in(rng, 6)
    for position, parts in split:
        draws = jnp.exp(jax.random.uniform(jax.random.fold_in(own, position), (parts,), jnp.float32, low / len(split), top_value / len(split)))
        loudness = loudness * jnp.repeat(draws, shape[position] // parts).reshape([-1 if axis == position else 1 for axis in range(len(shape))])
    return loudness


def noise(key, extent, deviation, limit, cuts=(), kind=jnp.bfloat16):
    values = deviation * jax.random.normal(key, extent, jnp.float32)
    if cuts:
        values = values * steps_of(key, extent, cuts, -0.22, 0.18)
    return jnp.clip(values, -limit, limit).astype(kind)


def bell_draw_with(stream_key, extent, width, limit, shards, heavy, dtype=jnp.bfloat16):
    drawn = width * jax.random.normal(stream_key, extent, jnp.float32)
    if shards:
        drawn = drawn * steps_of(stream_key, extent, shards, -0.22, 0.18)
    return jnp.clip(with_spikes(drawn, jax.random.fold_in(stream_key, 3), *heavy), -limit, limit).astype(dtype)


def setup_inputs(seed: int = 0, part: int = 0) -> dict:
    keys = jax.random.split(jax.random.key(seed), 6)
    own_keys = jax.random.split(jax.random.fold_in(keys[5], part), 6)
    taps = bell_draw_with(own_keys[0], (TOKENS, TAPS), 1.0, 6.0, ((1, 16),), (1, 0, 16, 2.0))
    w_join = noise(keys[1], (TAPS, HID), TAPS ** -0.5, 0.0546875, ((0, 16),))
    w_down = noise(keys[2], (HID, RANK), HID ** -0.5, 0.09375)
    w_up = noise(keys[3], (RANK, HID), RANK ** -0.5, 0.75)
    upstream = noise(own_keys[4], (TOKENS, STEPS * HID), 1.0, 6.0, ((0, 16),))
    return {"taps": taps, "w_join": w_join, "w_down": w_down, "w_up": w_up, "upstream": upstream}


def drafter(joined, w_down, w_up, upstream):
    out_width = w_up.shape[1]
    state = joined.astype(jnp.float32)
    saved = []
    outputs = []
    for section_index in range(STEPS):
        inv_norm = lax.rsqrt(lax.optimization_barrier(jnp.mean(state * state, axis=-1, keepdims=True)) + 1e-06)
        normed = (state * inv_norm).astype(jnp.bfloat16)
        low_rows = jnp.dot(normed, w_down, preferred_element_type=jnp.float32).astype(jnp.bfloat16)
        pre_act = jnp.dot(low_rows, w_up, preferred_element_type=jnp.float32)
        saved.append((state, inv_norm, normed, low_rows, pre_act))
        state = state + jax.nn.silu(pre_act)
        outputs.append(state.astype(jnp.bfloat16))
    drafts = jnp.concatenate(outputs, axis=1)
    state_grad = jnp.zeros(state.shape, jnp.float32)
    down_grad = jnp.zeros(w_down.shape, jnp.float32)
    up_grad = jnp.zeros(w_up.shape, jnp.float32)
    for section_index in reversed(range(STEPS)):
        prior, inv_norm, normed, low_rows, pre_act = saved[section_index]
        block = upstream[:, section_index * out_width:(section_index + 1) * out_width]
        state_grad = state_grad + block.astype(jnp.float32)
        sigma = jax.nn.sigmoid(pre_act)
        act_grad = (state_grad * sigma * (1.0 + pre_act * (1.0 - sigma))).astype(jnp.bfloat16)
        up_grad = up_grad + lax.dot_general(low_rows, act_grad, (((0,), (0,)), ((), ())), preferred_element_type=jnp.float32)
        low_cot = lax.dot_general(act_grad, w_up, (((1,), (1,)), ((), ())), preferred_element_type=jnp.float32).astype(jnp.bfloat16)
        down_grad = down_grad + lax.dot_general(normed, low_cot, (((0,), (0,)), ((), ())), preferred_element_type=jnp.float32)
        back_grad = lax.dot_general(low_cot, w_down, (((1,), (1,)), ((), ())), preferred_element_type=jnp.float32)
        inner = lax.optimization_barrier(jnp.mean(back_grad * prior, axis=-1, keepdims=True))
        state_grad = state_grad + back_grad * inv_norm - prior * inv_norm * inv_norm * inv_norm * inner
    return (drafts, state_grad.astype(jnp.bfloat16), down_grad, up_grad)

def reference(taps, w_join, w_down, w_up, upstream):
    joined = jnp.dot(taps, w_join, preferred_element_type=jnp.float32).astype(jnp.bfloat16)
    drafts, joined_cot, down_grad, up_grad = drafter(joined, w_down, w_up, upstream)
    join_grad = lax.dot_general(taps, joined_cot, (((0,), (0,)), ((), ())), preferred_element_type=jnp.float32)
    return (drafts, join_grad, down_grad, up_grad)
```

```python
import functools

import jax
import jax.numpy as jnp
from jax import lax
from jax.experimental import pallas as pl
from jax.experimental.pallas import tpu as pltpu
from jax.sharding import PartitionSpec as P

STEPS = 3
CHUNKS = 4
GRAD_CHUNKS = 2
ROWS = 16
TILE = 512
MESH = pl.DeviceIdType.MESH
F32 = jnp.float32
BF16 = jnp.bfloat16


def nt_dot(a, b):
    return lax.dot_general(a, b, (((1,), (1,)), ((), ())), preferred_element_type=F32)


def tn_dot(a, b):
    return lax.dot_general(a, b, (((0,), (0,)), ((), ())), preferred_element_type=F32)


def axis_orders(levels):
    first = list(range(levels))
    second = [0, 2, 1] + first[3:] if levels > 2 else first
    return first, second


def block_at(order, position, levels):
    return sum(((position >> (levels - 1 - i)) & 1) << order[i] for i in range(levels))


def exchange_kernel(n, levels, taps_hbm, w_hbm, down_hbm, up_hbm, upstream_hbm,
                    drafts_ref, cot_hbm, tap_rows_ref, grads_ref,
                    taps, w, w_down, w_up, upstream,
                    acc, gather, joined, states, pres, normed, lows, acts, low_cots,
                    partial, grad_acc, grad_gather, *rest):
    out_bufs = rest[0:levels]
    in_bufs = rest[levels:2 * levels]
    grad_out = rest[2 * levels:3 * levels]
    grad_in = rest[3 * levels:4 * levels]
    (rs_send, rs_recv, ag_send, ag_recv, grs_send, grs_recv, gag_send, gag_recv,
     w_sem, small_sem, cot_sem) = rest[4 * levels:]
    me = lax.axis_index("tok")
    bits = [(me // 2 ** b) % 2 for b in range(levels)]
    partners = [me + (1 - 2 * bits[b]) * 2 ** b for b in range(levels)]
    orders = axis_orders(levels)
    chunks, _, _, cw = gather.shape
    hid = chunks * cw
    gcw = grad_gather.shape[3]

    def xor_me(p):
        return sum(((1 - bits[b]) if (p >> b) & 1 else bits[b]) * 2 ** b for b in range(levels))

    taps_copy = pltpu.make_async_copy(taps_hbm, taps, small_sem.at[0])
    taps_copy.start()
    w_copies = [
        pltpu.make_async_copy(w_hbm.at[:, pl.ds(c * cw, cw)], w.at[c], w_sem.at[c])
        for c in range(chunks)
    ]
    for copy in w_copies:
        copy.start()
    small = [
        pltpu.make_async_copy(src, dst, small_sem.at[1 + i])
        for i, (src, dst) in enumerate(((down_hbm, w_down), (up_hbm, w_up), (upstream_hbm, upstream)))
    ]
    for copy in small:
        copy.start()

    barrier = pltpu.get_barrier_semaphore()
    for b in range(levels):
        pl.semaphore_signal(barrier, inc=1, device_id={"tok": partners[b]}, device_id_type=MESH)

    taps_copy.wait()
    for o, order in enumerate(orders):
        for q in range(n):
            tap_rows_ref[o, pl.ds(q * ROWS, ROWS), :] = taps[xor_me(block_at(order, q, levels))]
    pl.semaphore_wait(barrier, levels)

    pending = []

    def remote(src, dst, send, recv, b):
        copy = pltpu.make_async_remote_copy(
            src_ref=src, dst_ref=dst, send_sem=send, recv_sem=recv,
            device_id={"tok": partners[b]}, device_id_type=MESH)
        copy.start()
        pending.append(copy)
        return copy

    half = n // 2
    rs = {}

    def order_of(c):
        return orders[c % 2]

    def rs_stage(i, c, accs, outs, ins, send, recv, table):
        m = n >> i
        h = m // 2
        table[i - 1, c].wait_recv()
        got = ins[i - 1]
        outs[i][c] = (accs[c, h:m] + got[c, h:m].astype(F32)).astype(BF16)
        table[i, c] = remote(outs[i].at[c], ins[i].at[c], send.at[i, c], recv.at[i, c], order_of(c)[i])
        accs[c, 0:h] = accs[c, 0:h] + got[c, 0:h].astype(F32)

    def rs_last(c, accs, ins, table):
        table[levels - 1, c].wait_recv()
        return accs[c, 0] + ins[levels - 1][c, 0].astype(F32)

    def join_stage(i, c):
        if i == 0:
            w_copies[c].wait()
            tw = min(TILE, cw)
            for j in range(cw // tw):
                cols = slice(j * tw, (j + 1) * tw)
                tile = w[c, :, cols]
                away = jnp.dot(tap_rows_ref[c % 2, half * ROWS:, :], tile, preferred_element_type=F32)
                out_bufs[0][c, :, :, cols] = away.astype(BF16).reshape(half, ROWS, tw)
                kept = jnp.dot(tap_rows_ref[c % 2, :half * ROWS, :], tile, preferred_element_type=F32)
                acc[c, :, :, cols] = kept.reshape(half, ROWS, tw)
            rs[0, c] = remote(out_bufs[0].at[c], in_bufs[0].at[c], rs_send.at[0, c], rs_recv.at[0, c],
                              order_of(c)[0])
        elif i < levels:
            rs_stage(i, c, acc, out_bufs, in_bufs, rs_send, rs_recv, rs)
        else:
            joined[:, c * cw:(c + 1) * cw] = rs_last(c, acc, in_bufs, rs).astype(BF16)

    steps = sorted((c + 2 * i, -i, i, c) for i in range(levels + 1) for c in range(chunks))
    for _, _, i, c in steps:
        join_stage(i, c)

    for copy in small:
        copy.wait()

    def inverse_norm(state):
        return lax.rsqrt(jnp.mean(state * state, axis=-1, keepdims=True) + 1e-06)

    state = joined[...].astype(F32)
    invs = []
    for s in range(STEPS):
        states[s] = state
        inv = inverse_norm(state)
        invs.append(inv)
        rows = (state * inv).astype(BF16)
        normed[s * ROWS:(s + 1) * ROWS, :] = rows
        low = jnp.dot(rows, w_down[...], preferred_element_type=F32).astype(BF16)
        lows[s * ROWS:(s + 1) * ROWS, :] = low
        pre = jnp.dot(low, w_up[...], preferred_element_type=F32)
        pres[s] = pre
        state = states[s] + pre * jax.nn.sigmoid(pre)
        drafts_ref[:, s * hid:(s + 1) * hid] = state.astype(BF16)

    g = jnp.zeros((ROWS, hid), F32)
    for s in reversed(range(STEPS)):
        inv = invs[s]
        g = g + upstream[:, s * hid:(s + 1) * hid].astype(F32)
        pre = pres[s]
        sigma = jax.nn.sigmoid(pre)
        act = (g * sigma * (1.0 + pre * (1.0 - sigma))).astype(BF16)
        acts[s * ROWS:(s + 1) * ROWS, :] = act
        low_cot = nt_dot(act, w_up[...]).astype(BF16)
        low_cots[s * ROWS:(s + 1) * ROWS, :] = low_cot
        back = nt_dot(low_cot, w_down[...])
        prior = states[s]
        inner = jnp.mean(back * prior, axis=-1, keepdims=True)
        g = g + back * inv - prior * (inv * inv * inv * inner)
    cot = g.astype(BF16)
    for c in range(chunks):
        gather[c, 0] = cot[:, c * cw:(c + 1) * cw]

    def ag_stage(i, c, buf, send, recv, table):
        m = n >> (i + 1)
        if i < levels - 1:
            table[i + 1, c].wait_recv()
        table[i, c] = remote(buf.at[c, pl.ds(0, m)], buf.at[c, pl.ds(m, m)], send.at[i, c], recv.at[i, c],
                             order_of(c)[i])

    ag, grs, gag = {}, {}, {}
    for c in range(chunks):
        ag_stage(levels - 1, c, gather, ag_send, ag_recv, ag)

    rank = w_up.shape[0]
    blocks = rank // ROWS
    gw = partial.shape[2]
    for j in range(hid // gw):
        cols = slice(j * gw, (j + 1) * gw)
        partial[2 * blocks * j:2 * blocks * j + blocks] = tn_dot(
            low_cots[...], normed[:, cols]).reshape(blocks, ROWS, gw)
        partial[2 * blocks * j + blocks:2 * blocks * (j + 1)] = tn_dot(
            lows[...], acts[:, cols]).reshape(blocks, ROWS, gw)

    def grad_stage(i, c):
        if i == 0:
            for q in range(half, n):
                d = xor_me(block_at(order_of(c), q, levels))
                grad_out[0][c, q - half] = partial[d, :, c * gcw:(c + 1) * gcw].astype(BF16)
            grs[0, c] = remote(grad_out[0].at[c], grad_in[0].at[c], grs_send.at[0, c], grs_recv.at[0, c],
                               order_of(c)[0])
            for q in range(half):
                d = xor_me(block_at(order_of(c), q, levels))
                grad_acc[c, q] = partial[d, :, c * gcw:(c + 1) * gcw]
        elif i < levels:
            rs_stage(i, c, grad_acc, grad_out, grad_in, grs_send, grs_recv, grs)
        else:
            grad_gather[c, 0] = rs_last(c, grad_acc, grad_in, grs).astype(BF16)
            ag_stage(levels - 1, c, grad_gather, gag_send, gag_recv, gag)

    for i in range(levels):
        for c in range(GRAD_CHUNKS):
            grad_stage(i, c)
        if i < levels - 1:
            for c in range(chunks):
                ag_stage(levels - 2 - i, c, gather, ag_send, ag_recv, ag)
    for c in range(GRAD_CHUNKS):
        grad_stage(levels, c)
    cot_copies = []
    for c in range(chunks):
        ag[0, c].wait_recv()
        copy = pltpu.make_async_copy(gather.at[c], cot_hbm.at[c], cot_sem.at[c])
        copy.start()
        cot_copies.append(copy)
    for i in reversed(range(levels - 1)):
        for c in range(GRAD_CHUNKS):
            ag_stage(i, c, grad_gather, gag_send, gag_recv, gag)
    for c in range(GRAD_CHUNKS):
        gag[0, c].wait_recv()
        for q in range(n):
            d = xor_me(block_at(order_of(c), q, levels))
            rows = pl.multiple_of((d % (2 * blocks)) * ROWS, ROWS)
            cols = pl.multiple_of((d // (2 * blocks)) * gw + c * gcw, 128)
            grads_ref[pl.ds(rows, ROWS), pl.ds(cols, gcw)] = grad_gather[c, q]
    for copy in pending:
        copy.wait_send()
    for copy in cot_copies:
        copy.wait()


def join_grad_kernel(rows_ref, cot_ref, grads_ref, out_ref, down_ref, up_ref):
    c = pl.program_id(0)
    out_ref[...] = tn_dot(rows_ref[c % 2], cot_ref[0])
    rank = up_ref.shape[0]
    grads = grads_ref[...].astype(F32)
    down_ref[...] = grads[:rank].T
    up_ref[...] = grads[rank:]


def local(n, taps, w_join, w_down, w_up, upstream):
    levels = n.bit_length() - 1
    tokens, features = taps.shape
    hid = w_join.shape[1]
    rank = w_up.shape[0]
    cw = hid // CHUNKS
    gw = 2 * rank * hid // (ROWS * n)
    gcw = gw // GRAD_CHUNKS
    half = n // 2
    any_spec = pl.BlockSpec(memory_space=pl.ANY)
    vmem_spec = pl.BlockSpec(memory_space=pltpu.VMEM)
    halves = [pltpu.VMEM((CHUNKS, n >> (i + 1), ROWS, cw), BF16) for i in range(levels)]
    grad_halves = [pltpu.VMEM((GRAD_CHUNKS, n >> (i + 1), ROWS, gcw), BF16) for i in range(levels)]
    dma = pltpu.SemaphoreType.DMA
    drafts, cot, tap_rows, grads = pl.pallas_call(
        functools.partial(exchange_kernel, n, levels),
        out_shape=(
            jax.ShapeDtypeStruct((ROWS, STEPS * hid), BF16),
            jax.ShapeDtypeStruct((CHUNKS, n, ROWS, cw), BF16),
            jax.ShapeDtypeStruct((2, tokens, features), BF16),
            jax.ShapeDtypeStruct((2 * rank, hid), BF16),
        ),
        in_specs=[any_spec] * 5,
        out_specs=(vmem_spec, any_spec, vmem_spec, vmem_spec),
        scratch_shapes=[
            pltpu.VMEM((n, ROWS, features), BF16),
            pltpu.VMEM((CHUNKS, features, cw), BF16),
            pltpu.VMEM((hid, rank), BF16),
            pltpu.VMEM((rank, hid), BF16),
            pltpu.VMEM((ROWS, STEPS * hid), BF16),
            pltpu.VMEM((CHUNKS, half, ROWS, cw), F32),
            pltpu.VMEM((CHUNKS, n, ROWS, cw), BF16),
            pltpu.VMEM((ROWS, hid), BF16),
            pltpu.VMEM((STEPS, ROWS, hid), F32),
            pltpu.VMEM((STEPS, ROWS, hid), F32),
            pltpu.VMEM((STEPS * ROWS, hid), BF16),
            pltpu.VMEM((STEPS * ROWS, rank), BF16),
            pltpu.VMEM((STEPS * ROWS, hid), BF16),
            pltpu.VMEM((STEPS * ROWS, rank), BF16),
            pltpu.VMEM((n, ROWS, gw), F32),
            pltpu.VMEM((GRAD_CHUNKS, half, ROWS, gcw), F32),
            pltpu.VMEM((GRAD_CHUNKS, n, ROWS, gcw), BF16),
            *halves, *halves, *grad_halves, *grad_halves,
            *[dma((levels, CHUNKS))] * 4,
            *[dma((levels, GRAD_CHUNKS))] * 4,
            dma((CHUNKS,)),
            dma((4,)),
            dma((CHUNKS,)),
        ],
        compiler_params=pltpu.CompilerParams(
            collective_id=0, has_side_effects=True, vmem_limit_bytes=60 * 1024 * 1024),
    )(taps.reshape(n, ROWS, features), w_join, w_down, w_up, upstream)
    tw = min(TILE, cw)
    per = cw // tw
    join_grad, down_grad, up_grad = pl.pallas_call(
        join_grad_kernel,
        grid=(CHUNKS, per),
        out_shape=(
            jax.ShapeDtypeStruct((features, hid), F32),
            jax.ShapeDtypeStruct((hid, rank), F32),
            jax.ShapeDtypeStruct((rank, hid), F32),
        ),
        in_specs=[
            pl.BlockSpec((2, tokens, features), lambda c, j: (0, 0, 0)),
            pl.BlockSpec((1, tokens, tw), lambda c, j: (c, 0, j)),
            pl.BlockSpec((2 * rank, tw), lambda c, j: (0, c * per + j)),
        ],
        out_specs=(
            pl.BlockSpec((features, tw), lambda c, j: (0, c * per + j)),
            pl.BlockSpec((tw, rank), lambda c, j: (c * per + j, 0)),
            pl.BlockSpec((rank, tw), lambda c, j: (0, c * per + j)),
        ),
        compiler_params=pltpu.CompilerParams(vmem_limit_bytes=48 * 1024 * 1024),
    )(tap_rows, cot.reshape(CHUNKS, tokens, cw), grads)
    return drafts, join_grad, down_grad, up_grad


def solution(mesh):
    in_specs = (P("groups", "tok"), P("tok", None), P(), P(), P(("groups", "tok"), None))
    out_specs = (
        P(("groups", "tok"), None),
        P("tok", "groups"),
        P("groups", None),
        P("groups", None),
    )
    return jax.shard_map(
        functools.partial(local, mesh.shape["tok"]), mesh=mesh, in_specs=in_specs, out_specs=out_specs,
        check_vma=False)
```

```python
import functools

import jax
import jax.numpy as jnp
from jax import lax
from jax.experimental import pallas as pl
from jax.experimental.pallas import tpu as pltpu
from jax.sharding import PartitionSpec as P

STEPS = 3
CHUNKS = 4
GRAD_CHUNKS = 2
ROWS = 16
JOIN_LAG = 8
COT_PACE = (0.01, 3.2)
GRAD_PACE = (0.01, 1.6)
TILE = 1024
MESH = pl.DeviceIdType.MESH
F32 = jnp.float32
BF16 = jnp.bfloat16


def nt_dot(a, b):
    return lax.dot_general(a, b, (((1,), (1,)), ((), ())), preferred_element_type=F32)


def tn_dot(a, b):
    return lax.dot_general(a, b, (((0,), (0,)), ((), ())), preferred_element_type=F32)


def order_index(c):
    return c % 2


def axis_orders(levels):
    first = list(range(levels))
    second = [0, 2, 1] + first[3:] if levels > 2 else first
    return first, second


def block_at(order, position, levels):
    return sum(((position >> (levels - 1 - i)) & 1) << order[i] for i in range(levels))


def exchange_kernel(n, levels, taps_hbm, w_hbm, down_hbm, up_hbm, upstream_hbm,
                    drafts_ref, cot_hbm, taps_t_ref, grads_ref,
                    taps, tap_rows, w, w_down, w_up, upstream,
                    acc, gather, joined, states, pres, normed, lows, acts, low_cots,
                    partial, grad_acc, grad_gather, *rest):
    out_bufs = rest[0:levels]
    in_bufs = rest[levels:2 * levels]
    grad_out = rest[2 * levels:3 * levels]
    grad_in = rest[3 * levels:4 * levels]
    (rs_send, rs_recv, ag_send, ag_recv, grs_send, grs_recv, gag_send, gag_recv,
     w_sem, small_sem, cot_sem) = rest[4 * levels:]
    me = lax.axis_index("tok")
    bits = [(me // 2 ** b) % 2 for b in range(levels)]
    partners = [me + (1 - 2 * bits[b]) * 2 ** b for b in range(levels)]
    orders = axis_orders(levels)
    chunks, _, _, cw = gather.shape
    hid = chunks * cw
    gcw = grad_gather.shape[3]

    def xor_me(p):
        return sum(((1 - bits[b]) if (p >> b) & 1 else bits[b]) * 2 ** b for b in range(levels))

    taps_copy = pltpu.make_async_copy(taps_hbm, taps, small_sem.at[0])
    taps_copy.start()
    w_copies = [
        pltpu.make_async_copy(w_hbm.at[:, pl.ds(c * cw, cw)], w.at[c], w_sem.at[c])
        for c in range(chunks)
    ]
    for copy in w_copies:
        copy.start()
    small = [
        pltpu.make_async_copy(src, dst, small_sem.at[1 + i])
        for i, (src, dst) in enumerate(((down_hbm, w_down), (up_hbm, w_up), (upstream_hbm, upstream)))
    ]
    for copy in small:
        copy.start()

    barrier = pltpu.get_barrier_semaphore()
    for b in range(levels):
        pl.semaphore_signal(barrier, inc=1, device_id={"tok": partners[b]}, device_id_type=MESH)

    taps_copy.wait()
    for o, order in enumerate(orders):
        for q in range(n):
            tap_rows[o, pl.ds(q * ROWS, ROWS), :] = taps[xor_me(block_at(order, q, levels))]
    pl.semaphore_wait(barrier, levels)

    pending = []

    def remote(src, dst, send, recv, b):
        copy = pltpu.make_async_remote_copy(
            src_ref=src, dst_ref=dst, send_sem=send, recv_sem=recv,
            device_id={"tok": partners[b]}, device_id_type=MESH)
        copy.start()
        pending.append(copy)
        return copy

    half = n // 2
    rs = {}

    def order_of(c):
        return orders[order_index(c)]

    def rs_stage(i, c, accs, outs, ins, send, recv, table):
        m = n >> i
        h = m // 2
        table[i - 1, c].wait_recv()
        got = ins[i - 1]
        outs[i][c] = (accs[c, h:m] + got[c, h:m].astype(F32)).astype(BF16)
        table[i, c] = remote(outs[i].at[c], ins[i].at[c], send.at[i, c], recv.at[i, c], order_of(c)[i])
        accs[c, 0:h] = accs[c, 0:h] + got[c, 0:h].astype(F32)

    def rs_last(c, accs, ins, table):
        table[levels - 1, c].wait_recv()
        return accs[c, 0] + ins[levels - 1][c, 0].astype(F32)

    def join_stage(i, c):
        if i == 0:
            w_copies[c].wait()
            tw = min(512, cw)
            for j in range(cw // tw):
                cols = slice(j * tw, (j + 1) * tw)
                tile = w[c, :, cols]
                away = jnp.dot(tap_rows[order_index(c), half * ROWS:, :], tile, preferred_element_type=F32)
                out_bufs[0][c, :, :, cols] = away.astype(BF16).reshape(half, ROWS, tw)
                kept = jnp.dot(tap_rows[order_index(c), :half * ROWS, :], tile, preferred_element_type=F32)
                acc[c, :, :, cols] = kept.reshape(half, ROWS, tw)
            rs[0, c] = remote(out_bufs[0].at[c], in_bufs[0].at[c], rs_send.at[0, c], rs_recv.at[0, c],
                              order_of(c)[0])
        elif i < levels:
            rs_stage(i, c, acc, out_bufs, in_bufs, rs_send, rs_recv, rs)
        else:
            joined[:, c * cw:(c + 1) * cw] = rs_last(c, acc, in_bufs, rs).astype(BF16)

    steps = sorted((c + JOIN_LAG * i, -i, i, c) for i in range(levels + 1) for c in range(chunks))
    for at, (_, _, i, c) in enumerate(steps):
        if at == 2 * chunks:
            for o in range(2):
                taps_t_ref[o] = tap_rows[o].T
        join_stage(i, c)

    for copy in small:
        copy.wait()

    def inverse_norm(state):
        return lax.rsqrt(jnp.mean(state * state, axis=-1, keepdims=True) + 1e-06)

    state = joined[...].astype(F32)
    invs = []
    for s in range(STEPS):
        states[s] = state
        inv = inverse_norm(state)
        invs.append(inv)
        rows = (state * inv).astype(BF16)
        normed[s * ROWS:(s + 1) * ROWS, :] = rows
        low = nt_dot(rows, w_down[...]).astype(BF16)
        lows[s * ROWS:(s + 1) * ROWS, :] = low
        pre = jnp.dot(low, w_up[...], preferred_element_type=F32)
        pres[s] = pre
        state = states[s] + pre * jax.nn.sigmoid(pre)
        drafts_ref[:, s * hid:(s + 1) * hid] = state.astype(BF16)

    g = jnp.zeros((ROWS, hid), F32)
    for s in reversed(range(STEPS)):
        inv = invs[s]
        g = g + upstream[:, s * hid:(s + 1) * hid].astype(F32)
        pre = pres[s]
        sigma = jax.nn.sigmoid(pre)
        act = (g * sigma * (1.0 + pre * (1.0 - sigma))).astype(BF16)
        acts[s * ROWS:(s + 1) * ROWS, :] = act
        low_cot = nt_dot(act, w_up[...]).astype(BF16)
        low_cots[s * ROWS:(s + 1) * ROWS, :] = low_cot
        back = jnp.dot(low_cot, w_down[...], preferred_element_type=F32)
        prior = states[s]
        inner = jnp.mean(back * prior, axis=-1, keepdims=True)
        g = g + back * inv - prior * (inv * inv * inv * inner)
    cot = g.astype(BF16)
    for c in range(chunks):
        gather[c, 0] = cot[:, c * cw:(c + 1) * cw]

    def ag_stage(i, c, buf, send, recv, table):
        m = n >> (i + 1)
        if i < levels - 1:
            table[i + 1, c].wait_recv()
        table[i, c] = remote(buf.at[c, pl.ds(0, m)], buf.at[c, pl.ds(m, m)], send.at[i, c], recv.at[i, c],
                             order_of(c)[i])

    ag, grs, gag = {}, {}, {}
    for c in range(chunks):
        ag_stage(levels - 1, c, gather, ag_send, ag_recv, ag)

    rank = w_up.shape[0]
    blocks = rank // ROWS
    gw = partial.shape[2]
    for j in range(hid // gw):
        cols = slice(j * gw, (j + 1) * gw)
        partial[2 * blocks * j:2 * blocks * j + blocks] = tn_dot(
            low_cots[...], normed[:, cols]).reshape(blocks, ROWS, gw)
        partial[2 * blocks * j + blocks:2 * blocks * (j + 1)] = tn_dot(
            lows[...], acts[:, cols]).reshape(blocks, ROWS, gw)

    def grad_stage(i, c):
        if i == 0:
            for q in range(half, n):
                d = xor_me(block_at(order_of(c), q, levels))
                grad_out[0][c, q - half] = partial[d, :, c * gcw:(c + 1) * gcw].astype(BF16)
            grs[0, c] = remote(grad_out[0].at[c], grad_in[0].at[c], grs_send.at[0, c], grs_recv.at[0, c],
                               order_of(c)[0])
            for q in range(half):
                d = xor_me(block_at(order_of(c), q, levels))
                grad_acc[c, q] = partial[d, :, c * gcw:(c + 1) * gcw]
        elif i < levels:
            rs_stage(i, c, grad_acc, grad_out, grad_in, grs_send, grs_recv, grs)
        else:
            grad_gather[c, 0] = rs_last(c, grad_acc, grad_in, grs).astype(BF16)
            ag_stage(levels - 1, c, grad_gather, gag_send, gag_recv, gag)

    cot_copies = []

    def cot_stage(k, c):
        if k < levels:
            ag_stage(levels - 1 - k, c, gather, ag_send, ag_recv, ag)
        else:
            ag[0, c].wait_recv()
            copy = pltpu.make_async_copy(gather.at[c], cot_hbm.at[c], cot_sem.at[c])
            copy.start()
            cot_copies.append(copy)

    def grad_step(k, c):
        if k <= levels:
            grad_stage(k, c)
        elif k < 2 * levels:
            ag_stage(2 * levels - 1 - k, c, grad_gather, gag_send, gag_recv, gag)

    events = [(COT_PACE[0] * c + COT_PACE[1] * k, 1, k, c) for k in range(1, levels + 1) for c in range(chunks)]
    events += [(GRAD_PACE[0] * c + GRAD_PACE[1] * k, 0, k, c) for k in range(2 * levels) for c in range(GRAD_CHUNKS)]
    for _, kind, k, c in sorted(events):
        (cot_stage if kind else grad_step)(k, c)
    for c in range(GRAD_CHUNKS):
        gag[0, c].wait_recv()
        for q in range(n):
            d = xor_me(block_at(order_of(c), q, levels))
            rows = pl.multiple_of((d % (2 * blocks)) * ROWS, ROWS)
            cols = pl.multiple_of((d // (2 * blocks)) * gw + c * gcw, 128)
            grads_ref[pl.ds(rows, ROWS), pl.ds(cols, gcw)] = grad_gather[c, q]
    for copy in pending:
        copy.wait_send()
    for copy in cot_copies:
        copy.wait()


def join_grad_kernel(rows_ref, cot_ref, grads_ref, drafts_ref, out_ref, down_ref, up_ref, drafts_out_ref):
    drafts_out_ref[...] = drafts_ref[...]
    c = pl.program_id(0)
    out_ref[...] = jnp.dot(rows_ref[order_index(c)], cot_ref[0], preferred_element_type=F32)
    rank = up_ref.shape[0]
    grads = grads_ref[...].astype(F32)
    down_ref[...] = grads[:rank]
    up_ref[...] = grads[rank:]


def local(n, taps, w_join, w_down, w_up, upstream):
    levels = n.bit_length() - 1
    tokens, features = taps.shape
    hid = w_join.shape[1]
    rank = w_up.shape[0]
    cw = hid // CHUNKS
    gw = 2 * rank * hid // (ROWS * n)
    gcw = gw // GRAD_CHUNKS
    half = n // 2
    any_spec = pl.BlockSpec(memory_space=pl.ANY)
    vmem_spec = pl.BlockSpec(memory_space=pltpu.VMEM)
    halves = [pltpu.VMEM((CHUNKS, n >> (i + 1), ROWS, cw), BF16) for i in range(levels)]
    grad_halves = [pltpu.VMEM((GRAD_CHUNKS, n >> (i + 1), ROWS, gcw), BF16) for i in range(levels)]
    dma = pltpu.SemaphoreType.DMA
    drafts, cot, tap_rows, grads = pl.pallas_call(
        functools.partial(exchange_kernel, n, levels),
        out_shape=(
            jax.ShapeDtypeStruct((ROWS, STEPS * hid), BF16),
            jax.ShapeDtypeStruct((CHUNKS, n, ROWS, cw), BF16),
            jax.ShapeDtypeStruct((2, features, tokens), BF16),
            jax.ShapeDtypeStruct((2 * rank, hid), BF16),
        ),
        in_specs=[any_spec] * 5,
        out_specs=(vmem_spec, any_spec, vmem_spec, vmem_spec),
        scratch_shapes=[
            pltpu.VMEM((n, ROWS, features), BF16),
            pltpu.VMEM((2, tokens, features), BF16),
            pltpu.VMEM((CHUNKS, features, cw), BF16),
            pltpu.VMEM((rank, hid), BF16),
            pltpu.VMEM((rank, hid), BF16),
            pltpu.VMEM((ROWS, STEPS * hid), BF16),
            pltpu.VMEM((CHUNKS, half, ROWS, cw), F32),
            pltpu.VMEM((CHUNKS, n, ROWS, cw), BF16),
            pltpu.VMEM((ROWS, hid), BF16),
            pltpu.VMEM((STEPS, ROWS, hid), F32),
            pltpu.VMEM((STEPS, ROWS, hid), F32),
            pltpu.VMEM((STEPS * ROWS, hid), BF16),
            pltpu.VMEM((STEPS * ROWS, rank), BF16),
            pltpu.VMEM((STEPS * ROWS, hid), BF16),
            pltpu.VMEM((STEPS * ROWS, rank), BF16),
            pltpu.VMEM((n, ROWS, gw), F32),
            pltpu.VMEM((GRAD_CHUNKS, half, ROWS, gcw), F32),
            pltpu.VMEM((GRAD_CHUNKS, n, ROWS, gcw), BF16),
            *halves, *halves, *grad_halves, *grad_halves,
            *[dma((levels, CHUNKS))] * 4,
            *[dma((levels, GRAD_CHUNKS))] * 4,
            dma((CHUNKS,)),
            dma((4,)),
            dma((CHUNKS,)),
        ],
        compiler_params=pltpu.CompilerParams(
            collective_id=0, has_side_effects=True, vmem_limit_bytes=60 * 1024 * 1024),
    )(taps.reshape(n, ROWS, features), w_join, w_down.T, w_up, upstream)
    tw = min(TILE, cw)
    per = cw // tw
    dw = STEPS * hid // (CHUNKS * per)
    join_grad, down_grad, up_grad, drafts = pl.pallas_call(
        join_grad_kernel,
        grid=(CHUNKS, per),
        out_shape=(
            jax.ShapeDtypeStruct((features, hid), F32),
            jax.ShapeDtypeStruct((rank, hid), F32),
            jax.ShapeDtypeStruct((rank, hid), F32),
            jax.ShapeDtypeStruct((ROWS, STEPS * hid), BF16),
        ),
        in_specs=[
            pl.BlockSpec((2, features, tokens), lambda c, j: (0, 0, 0)),
            pl.BlockSpec((1, tokens, tw), lambda c, j: (c, 0, j)),
            pl.BlockSpec((2 * rank, tw), lambda c, j: (0, c * per + j)),
            pl.BlockSpec((ROWS, dw), lambda c, j: (0, c * per + j)),
        ],
        out_specs=(
            pl.BlockSpec((features, tw), lambda c, j: (0, c * per + j)),
            pl.BlockSpec((rank, tw), lambda c, j: (0, c * per + j)),
            pl.BlockSpec((rank, tw), lambda c, j: (0, c * per + j)),
            pl.BlockSpec((ROWS, dw), lambda c, j: (0, c * per + j)),
        ),
        compiler_params=pltpu.CompilerParams(vmem_limit_bytes=60 * 1024 * 1024),
    )(tap_rows, cot.reshape(CHUNKS, tokens, cw), grads, drafts)
    return drafts, join_grad, down_grad.T, up_grad


def solution(mesh):
    in_specs = (P("groups", "tok"), P("tok", None), P(), P(), P(("groups", "tok"), None))
    out_specs = (
        P(("groups", "tok"), None),
        P("tok", "groups"),
        P("groups", None),
        P("groups", None),
    )
    return jax.shard_map(
        functools.partial(local, mesh.shape["tok"]), mesh=mesh, in_specs=in_specs, out_specs=out_specs,
        check_vma=False)
```
